32 devices in a mesh: wide: 4 (over z), grp: 8 (over y, x, core).
Axes of the slice: x: 2, y: 2, z: 4, core: 2. Of those that a mesh axis runs over, the one named last changes fastest.
Arguments:
- amplitudes: bfloat16 [32, 8192], P(('wide', 'grp')), may hold values from -6 to 6
- amplitude_live: int32 [32, 64], replicated, may hold values from 0 to 1, as said below
- integrals: bfloat16 [2048, 8192], P('grp', 'wide'), may hold values from -0.09375 to 0.09375
- integral_live: int32 [16, 64], P('grp', 'wide'), may hold values 0 or 1
Outputs:
- ladder: bfloat16 [32, 2048], P(('wide', 'grp'))
The draws below stay inside these ranges and needn't reach their ends.
Inputs may be any that keep to these rules, and one draw needn't show every extreme that they name: `amplitude_live`: entries are 0 or 1. In every row b, among the 16 cd tiles c with c // 16 equal to one index of wide, at most 12 are 1; in every row exactly 12 for at least one such index.
All inputs are finite; a program needn't handle non-finite values. No bound on the sum of `integral_live` on one device may be relied on, other than what follows from the above.
Results may differ from the reference program's by a relative error of at most 0.0018.
Values may be sent and summed in bfloat16 or wider, within the bound.
A program may use at most 64 MiB of HBM per device.

```python
import jax
import jax.numpy as jnp
from jax import lax

TW = 128
ROWS_DEV = 1
CD_DEV = 16
CAP = 12
NBLK = 32
IJ = 32
NCD = 64
NAB = 16
N_WIDE = 4


def draw_amplitude_live(key, part):
    key_score = jax.random.fold_in(key, 11)
    key_count = jax.random.fold_in(key, 12)
    key_full = jax.random.fold_in(key, 13)
    scores = jax.random.randint(key_score, (NBLK, N_WIDE, CD_DEV), 0, 65536) * CD_DEV + jnp.arange(CD_DEV, dtype=jnp.int32)
    ranking = jnp.argsort(jnp.argsort(scores, axis=-1), axis=-1)
    counts = jax.random.randint(key_count, (NBLK, N_WIDE), 1, CAP + 1)
    fullest = jax.random.randint(key_full, (NBLK, 1), 0, N_WIDE)
    counts = jnp.where(jnp.arange(N_WIDE, dtype=jnp.int32)[None, :] == fullest, CAP, counts)
    live = (ranking < counts[:, :, None]).astype(jnp.int32)
    return live.reshape(NBLK, N_WIDE * CD_DEV)


def with_ends(values, key, smallest, top_value):
    index_at = [jax.random.randint(jax.random.fold_in(key, axis), (), 0, length) for axis, length in enumerate(values.shape)]
    main_axis = values.shape.index(max(values.shape))
    beside = index_at[:main_axis] + [(index_at[main_axis] + 1) % values.shape[main_axis]] + index_at[main_axis + 1:]
    return values.at[tuple(index_at)].set(smallest).at[tuple(beside)].set(top_value)


def steps_of(stream_key, dims, split, low, top_value):
    gain, own = 1.0, jax.random.fold_in(stream_key, 6)
    for position, parts in split:
        steps = jnp.exp(jax.random.uniform(jax.random.fold_in(own, position), (parts,), jnp.float32, low / len(split), top_value / len(split)))
        gain = gain * jnp.repeat(steps, dims[position] // parts).reshape([-1 if axis == position else 1 for axis in range(len(dims))])
    return gain


def normal_values(key, dims, scale, most, pieces=(), held_as=jnp.bfloat16):
    drawn = jax.random.normal(key, dims, jnp.float32) * scale
    if len(pieces) > 0:
        drawn = steps_of(key, dims, pieces, -0.22, 0.18) * drawn
    return jnp.clip(drawn, min=-most, max=most).astype(held_as)


def setup_inputs(seed: int = 0) -> dict:
    key_of = jax.random.split(jax.random.key(seed), 5)
    amplitudes = normal_values(key_of[0], (IJ, NCD * TW), 1.0, 6.0, ((0, 32),))
    amplitude_live = draw_amplitude_live(jax.random.fold_in(key_of[4], 71), 0)
    integrals = normal_values(key_of[2], (NAB * TW, NCD * TW), (NCD * TW // 2) ** -0.5, 0.09375, ((0, 8), (1, 4)))
    integral_live = with_ends((jax.random.randint(key_of[3], (NAB, NCD), 0, 4) < 3).astype(jnp.int32), jax.random.fold_in(key_of[3], 1), 0, 1)
    return {"amplitudes": amplitudes, "amplitude_live": amplitude_live, "integrals": integrals, "integral_live": integral_live}


def reference(amplitudes, amplitude_live, integrals, integral_live):
    amp_mask = amplitude_live.astype(amplitudes.dtype)
    amp_used = (amplitudes.reshape(NBLK, ROWS_DEV, NCD, TW) * amp_mask[:, None, :, None]).reshape(IJ, NCD * TW)
    int_mask = integral_live.astype(integrals.dtype)
    int_used = (integrals.reshape(NAB, TW, NCD, TW) * int_mask[:, None, :, None]).reshape(NAB * TW, NCD * TW)
    ladder = lax.dot_general(amp_used, int_used, (((1,), (1,)), ((), ())), preferred_element_type=jnp.float32)
    return ladder.astype(jnp.bfloat16)
```

```python
import functools

import jax
import jax.numpy as jnp
from jax import lax
from jax.experimental import pallas as pl
from jax.experimental.pallas import tpu as pltpu
from jax.sharding import PartitionSpec as P

TW = 128
MESH = pl.DeviceIdType.MESH


def loop(count, body, limit=32):
    if count <= limit:
        for i in range(count):
            body(i)
    else:
        lax.fori_loop(0, count, lambda i, c: (body(i), c)[1], 0)


def kernel(
    n_wide, n_grp,
    amp_hbm, live_hbm, int_hbm, int_live_hbm, out_ref,
    amp, live, ints, int_live, tiles, send_buf, recv_buf, wide_tiles, lhs,
    partial, rows_in,
    load_sems, send_sem, recv_sem, send2_sem, recv2_sem,
):
    n = n_wide * n_grp
    cd_tiles = ints.shape[1] // TW
    ab_tiles = ints.shape[0] // TW
    ab = ints.shape[0]
    wide = lax.axis_index("wide")
    grp = lax.axis_index("grp")
    me = wide * n_grp + grp

    slab = pl.multiple_of((me // 8) * 8, 8)
    loads = [
        pltpu.make_async_copy(amp_hbm, amp, load_sems.at[0]),
        pltpu.make_async_copy(live_hbm.at[pl.ds(slab, 8), :], live, load_sems.at[1]),
        pltpu.make_async_copy(int_live_hbm, int_live, load_sems.at[2]),
        pltpu.make_async_copy(int_hbm, ints, load_sems.at[3]),
    ]
    for load in loads:
        load.start()

    barrier = pltpu.get_barrier_semaphore()

    def place(i):
        other = lax.rem(me + i, n)
        return other, (other // n_grp, lax.rem(other, n_grp))

    def greet(i):
        _, where = place(i + 1)
        pl.semaphore_signal(barrier, inc=1, device_id=where, device_id_type=MESH)

    loop(n - 1, greet)

    loads[0].wait()
    loads[1].wait()
    my_row = lax.rem(me, 8)

    def prepare(w):
        for c in range(cd_tiles):
            t = w * cd_tiles + c
            column = t * TW if isinstance(w, int) else pl.multiple_of(t * TW, TW)
            row = amp[:, pl.ds(column, TW)].astype(jnp.float32)
            tiles[c:c + 1, :] = row * live[my_row, t].astype(jnp.float32)
        send_buf[w] = tiles[...].astype(jnp.bfloat16)

    loop(n_wide, prepare, 4)

    pl.semaphore_wait(barrier, n - 1)

    def send(i):
        other, where = place(i + 1)
        pltpu.make_async_remote_copy(
            src_ref=send_buf.at[other // n_grp],
            dst_ref=recv_buf.at[me],
            send_sem=send_sem,
            recv_sem=recv_sem,
            device_id=where,
            device_id_type=MESH,
        ).start()

    loop(n - 1, send)
    recv_buf[me] = send_buf[wide]

    loads[2].wait()
    loads[3].wait()
    for a in range(ab_tiles):
        for c in range(cd_tiles):
            block = (slice(a * TW, (a + 1) * TW), slice(c * TW, (c + 1) * TW))
            keep = jnp.full((TW, TW), int_live[a, c].astype(jnp.float32), jnp.float32)
            ints[block] = ints[block] * keep.astype(jnp.bfloat16)

    others = recv_buf.at[pl.ds(0, n - 1)]
    pltpu.make_async_copy(others, others, recv_sem).wait()

    step = min(n, 32)

    def multiply(r):
        first = r * step
        wide_tiles[...] = (
            recv_buf[pl.ds(first, step)].astype(jnp.float32).reshape(step * cd_tiles, TW)
        )
        for c in range(cd_tiles):
            lhs[:, c * TW:(c + 1) * TW] = wide_tiles[
                pl.ds(c, step, stride=cd_tiles), :
            ].astype(jnp.bfloat16)
        total = lax.dot_general(
            lhs[...], ints[...], (((1,), (1,)), ((), ())),
            preferred_element_type=jnp.float32,
        )
        partial[pl.ds(first, step)] = total.reshape(step, 1, ab)

    loop(n // step, multiply, 1)

    def send_row(i):
        other, where = place(i + 1)
        pltpu.make_async_remote_copy(
            src_ref=partial.at[other],
            dst_ref=rows_in.at[me],
            send_sem=send2_sem,
            recv_sem=recv2_sem,
            device_id=where,
            device_id_type=MESH,
        ).start()

    loop(n - 1, send_row)
    rows_in[me] = partial[me]
    other_rows = rows_in.at[pl.ds(0, n - 1)]
    pltpu.make_async_copy(other_rows, other_rows, recv2_sem).wait()

    for g in range(n_grp):
        if n_wide <= 8:
            total = rows_in[g]
            for w in range(1, n_wide):
                total = total + rows_in[w * n_grp + g]
        else:
            total = lax.fori_loop(
                1, n_wide, lambda w, s: s + rows_in[w * n_grp + g], rows_in[g]
            )
        out_ref[:, g * ab:(g + 1) * ab] = total.astype(jnp.bfloat16)

    pltpu.make_async_copy(others, others, send_sem).wait()
    pltpu.make_async_copy(other_rows, other_rows, send2_sem).wait()


def per_device(amplitudes, amplitude_live, integrals, integral_live):
    n_wide = lax.axis_size("wide")
    n_grp = lax.axis_size("grp")
    n = n_wide * n_grp
    ab, cd = integrals.shape
    cd_tiles = cd // TW
    step = min(n, 32)
    bf16, f32 = jnp.bfloat16, jnp.float32
    anywhere = pl.BlockSpec(memory_space=pl.ANY)
    return pl.pallas_call(
        functools.partial(kernel, n_wide, n_grp),
        out_shape=jax.ShapeDtypeStruct((1, n_grp * ab), bf16),
        in_specs=[anywhere] * 4,
        out_specs=pl.BlockSpec(memory_space=pltpu.VMEM),
        scratch_shapes=[
            pltpu.VMEM(amplitudes.shape, bf16),
            pltpu.SMEM((8, amplitude_live.shape[1]), jnp.int32),
            pltpu.VMEM((ab, cd), bf16),
            pltpu.SMEM(integral_live.shape, jnp.int32),
            pltpu.VMEM((cd_tiles, TW), f32),
            pltpu.VMEM((n_wide, cd_tiles, TW), bf16),
            pltpu.VMEM((n, cd_tiles, TW), bf16),
            pltpu.VMEM((step * cd_tiles, TW), f32),
            pltpu.VMEM((step, cd), bf16),
            pltpu.VMEM((n, 1, ab), f32),
            pltpu.VMEM((n, 1, ab), f32),
            pltpu.SemaphoreType.DMA((4,)),
            pltpu.SemaphoreType.DMA,
            pltpu.SemaphoreType.DMA,
            pltpu.SemaphoreType.DMA,
            pltpu.SemaphoreType.DMA,
        ],
        compiler_params=pltpu.CompilerParams(
            collective_id=0, has_side_effects=True, vmem_limit_bytes=48 * 1024 * 1024
        ),
        cost_estimate=pl.CostEstimate(
            flops=2 * n * ab * cd, bytes_accessed=2 * ab * cd, transcendentals=0
        ),
    )(amplitudes, amplitude_live, integrals, integral_live)


def solution(mesh):
    in_specs = (P(("wide", "grp"), None), P(), P("grp", "wide"), P("grp", "wide"))
    out_specs = P(("wide", "grp"), None)
    return jax.shard_map(
        per_device, mesh=mesh, in_specs=in_specs, out_specs=out_specs, check_vma=False
    )
```

```python
import functools

import jax
import jax.numpy as jnp
from jax import lax
from jax.experimental import pallas as pl
from jax.experimental.pallas import tpu as pltpu
from jax.sharding import PartitionSpec as P

TW = 128
MESH = pl.DeviceIdType.MESH


def loop(count, body, limit):
    if count <= limit:
        for i in range(count):
            body(i)
    else:
        lax.fori_loop(0, count, lambda i, c: (body(i), c)[1], 0)


def kernel(
    n_wide, n_grp,
    amp_hbm, live_hbm, int_hbm, int_live_hbm, out_ref,
    amp, live, ints, int_live, tiles, send_buf, blocks, wide_tiles, lhs,
    partial, slabs, rows,
    load_sems, send_sems, recv_sems,
):
    ab, cd = ints.shape
    cd_tiles, ab_tiles = cd // TW, ab // TW
    wide = lax.axis_index("wide")
    grp = lax.axis_index("grp")
    my_row = lax.rem(wide * n_grp + grp, 8)

    slab = pl.multiple_of(((wide * n_grp + grp) // 8) * 8, 8)
    loads = [
        pltpu.make_async_copy(amp_hbm, amp, load_sems.at[0]),
        pltpu.make_async_copy(live_hbm.at[pl.ds(slab, 8), :], live, load_sems.at[1]),
        pltpu.make_async_copy(int_live_hbm, int_live, load_sems.at[2]),
        pltpu.make_async_copy(int_hbm, ints, load_sems.at[3]),
    ]
    for load in loads:
        load.start()

    barrier = pltpu.get_barrier_semaphore()

    def after(index, i, count):
        there = index + i
        return jnp.where(there >= count, there - count, there)

    def over_wide(body):
        def one(i):
            there = after(wide, i + 1, n_wide)
            body(there, (there, grp))
        loop(n_wide - 1, one, 8)

    def over_grp(body):
        for i in range(1, n_grp):
            there = after(grp, i, n_grp)
            body(there, (wide, there))

    def greet(_, where):
        pl.semaphore_signal(barrier, inc=1, device_id=where, device_id_type=MESH)

    over_wide(greet)
    over_grp(greet)

    loads[0].wait()
    loads[1].wait()

    def prepare(w):
        for c in range(cd_tiles):
            t = w * cd_tiles + c
            column = t * TW if isinstance(w, int) else pl.multiple_of(t * TW, TW)
            row = amp[:, pl.ds(column, TW)].astype(jnp.float32)
            tiles[c:c + 1, :] = row * live[my_row, t].astype(jnp.float32)
        send_buf[w] = tiles[...].astype(jnp.bfloat16)

    loop(n_wide, prepare, 4)

    pl.semaphore_wait(barrier, n_wide + n_grp - 2)

    def send(stage, src, dst, where):
        pltpu.make_async_remote_copy(
            src_ref=src,
            dst_ref=dst,
            send_sem=send_sems.at[stage],
            recv_sem=recv_sems.at[stage],
            device_id=where,
            device_id_type=MESH,
        ).start()

    def wait_all(refs, sem):
        pltpu.make_async_copy(refs, refs, sem).wait()

    over_wide(lambda w, where: send(0, send_buf.at[w], blocks.at[grp, wide], where))
    blocks[grp, wide] = send_buf[wide]

    loads[2].wait()
    loads[3].wait()
    for a in range(ab_tiles):
        for c in range(cd_tiles):
            block = (slice(a * TW, (a + 1) * TW), slice(c * TW, (c + 1) * TW))
            keep = jnp.full((TW, TW), int_live[a, c].astype(jnp.float32), jnp.float32)
            ints[block] = ints[block] * keep.astype(jnp.bfloat16)

    from_wide = blocks.at[0, pl.ds(0, n_wide - 1)]
    wait_all(from_wide, recv_sems.at[0])
    over_grp(lambda _, where: send(1, blocks.at[grp], blocks.at[grp], where))
    from_grp = blocks.at[pl.ds(0, n_grp - 1)]
    wait_all(from_grp, recv_sems.at[1])

    step = min(n_wide, 4)

    def multiply(r):
        first = r * step
        for g in range(n_grp):
            wide_tiles[g] = (
                blocks[g, pl.ds(first, step)].astype(jnp.float32).reshape(step * cd_tiles, TW)
            )
        flat = wide_tiles.reshape(n_grp * step * cd_tiles, TW)
        for w in range(step):
            for c in range(0, cd_tiles):
                lhs[w * n_grp:(w + 1) * n_grp, c * TW:(c + 1) * TW] = flat[
                    pl.ds(w * cd_tiles + c, n_grp, stride=step * cd_tiles), :
                ]
        total = lax.dot_general(
            lhs[...].astype(jnp.bfloat16), ints[...], (((1,), (1,)), ((), ())),
            preferred_element_type=jnp.float32,
        )
        partial[pl.ds(first, step)] = total.reshape(step, n_grp, ab)

    loop(n_wide // step, multiply, 1)

    over_wide(lambda w, where: send(2, partial.at[w], slabs.at[wide], where))
    slabs[wide] = partial[wide]
    from_wide_slabs = slabs.at[pl.ds(0, n_wide - 1)]
    wait_all(from_wide_slabs, recv_sems.at[2])
    if n_wide <= 8:
        total = slabs[0]
        for w in range(1, n_wide):
            total = total + slabs[w]
    else:
        total = lax.fori_loop(1, n_wide, lambda w, s: s + slabs[w], slabs[0])
    for g in range(n_grp):
        rows[g] = total[g:g + 1, :]
    columns = pl.ds(pl.multiple_of(grp * ab, ab), ab)
    own = pltpu.make_async_copy(rows.at[grp], out_ref.at[:, columns], load_sems.at[0])
    own.start()
    over_grp(lambda g, where: send(3, rows.at[g], out_ref.at[:, columns], where))
    from_grp_rows = out_ref.at[:, pl.ds(0, (n_grp - 1) * ab)]
    wait_all(from_grp_rows, recv_sems.at[3])
    own.wait()

    wait_all(from_wide, send_sems.at[0])
    wait_all(from_grp, send_sems.at[1])
    wait_all(from_wide_slabs, send_sems.at[2])
    wait_all(rows.at[pl.ds(0, n_grp - 1)], send_sems.at[3])


def per_device(amplitudes, amplitude_live, integrals, integral_live):
    n_wide = lax.axis_size("wide")
    n_grp = lax.axis_size("grp")
    ab, cd = integrals.shape
    cd_tiles = cd // TW
    step = min(n_wide, 4)
    bf16, f32 = jnp.bfloat16, jnp.float32
    anywhere = pl.BlockSpec(memory_space=pl.ANY)
    finished = pl.pallas_call(
        functools.partial(kernel, n_wide, n_grp),
        out_shape=jax.ShapeDtypeStruct((1, n_grp * ab), f32),
        in_specs=[anywhere] * 4,
        out_specs=anywhere,
        scratch_shapes=[
            pltpu.VMEM(amplitudes.shape, bf16),
            pltpu.SMEM((8, amplitude_live.shape[1]), jnp.int32),
            pltpu.VMEM((ab, cd), bf16),
            pltpu.SMEM(integral_live.shape, jnp.int32),
            pltpu.VMEM((cd_tiles, TW), f32),
            pltpu.VMEM((n_wide, cd_tiles, TW), bf16),
            pltpu.VMEM((n_grp, n_wide, cd_tiles, TW), bf16),
            pltpu.VMEM((n_grp, step * cd_tiles, TW), f32),
            pltpu.VMEM((n_grp * step, cd), f32),
            pltpu.VMEM((n_wide, n_grp, ab), f32),
            pltpu.VMEM((n_wide, n_grp, ab), f32),
            pltpu.VMEM((n_grp, 1, ab), f32),
            pltpu.SemaphoreType.DMA((4,)),
            pltpu.SemaphoreType.DMA((4,)),
            pltpu.SemaphoreType.DMA((4,)),
        ],
        compiler_params=pltpu.CompilerParams(
            collective_id=0, has_side_effects=True, vmem_limit_bytes=60 * 1024 * 1024
        ),
        cost_estimate=pl.CostEstimate(
            flops=2 * n_wide * n_grp * ab * cd, bytes_accessed=2 * ab * cd, transcendentals=0
        ),
    )(amplitudes, amplitude_live, integrals, integral_live)
    return finished.astype(bf16)


def solution(mesh):
    in_specs = (P(("wide", "grp"), None), P(), P("grp", "wide"), P("grp", "wide"))
    out_specs = P(("wide", "grp"), None)
    return jax.shard_map(
        per_device, mesh=mesh, in_specs=in_specs, out_specs=out_specs, check_vma=False
    )
```

```python
import functools

import jax
import jax.numpy as jnp
from jax import lax
from jax.experimental import pallas as pl
from jax.experimental.pallas import tpu as pltpu
from jax.sharding import PartitionSpec as P

TW = 128
MESH = pl.DeviceIdType.MESH


def loop(count, body, limit):
    if count <= limit:
        for i in range(count):
            body(i)
    else:
        lax.fori_loop(0, count, lambda i, c: (body(i), c)[1], 0)


def kernel(
    n_wide, n_grp,
    amp_hbm, live_hbm, int_hbm, int_live_hbm, out_ref,
    amp, live, ints, int_live, tiles, send_buf, blocks, wide_tiles, lhs,
    partial, rows_in,
    load_sems, recv_sems, row_sem, send_sems,
):
    ab, cd = ints.shape
    cd_tiles, ab_tiles = cd // TW, ab // TW
    wide = lax.axis_index("wide")
    grp = lax.axis_index("grp")
    my_row = lax.rem(wide * n_grp + grp, 8)

    slab = pl.multiple_of(((wide * n_grp + grp) // 8) * 8, 8)
    loads = [
        pltpu.make_async_copy(amp_hbm, amp, load_sems.at[0]),
        pltpu.make_async_copy(live_hbm.at[pl.ds(slab, 8), :], live, load_sems.at[1]),
        pltpu.make_async_copy(int_live_hbm, int_live, load_sems.at[2]),
        pltpu.make_async_copy(int_hbm, ints, load_sems.at[3]),
    ]
    for load in loads:
        load.start()

    barrier = pltpu.get_barrier_semaphore()

    def up(index, i, count):
        there = index + i
        return jnp.where(there >= count, there - count, there)

    def down(index, i, count):
        there = index - i
        return jnp.where(there < 0, there + count, there)

    near = [up(grp, i, n_grp) for i in range(n_grp)]

    def plane(w, body, first):
        for g in near[first:]:
            body(w, g)

    def greet(w, g):
        pl.semaphore_signal(barrier, inc=1, device_id=(w, g), device_id_type=MESH)

    loop(n_wide - 1, lambda i: plane(up(wide, i + 1, n_wide), greet, 0), 8)
    plane(wide, greet, 1)

    loads[0].wait()
    loads[1].wait()

    def prepare(w):
        for c in range(cd_tiles):
            t = w * cd_tiles + c
            column = t * TW if isinstance(w, int) else pl.multiple_of(t * TW, TW)
            row = amp[:, pl.ds(column, TW)].astype(jnp.float32)
            tiles[c:c + 1, :] = row * live[my_row, t].astype(jnp.float32)
        send_buf[w] = tiles[...].astype(jnp.bfloat16)

    loop(n_wide, prepare, 4)

    pl.semaphore_wait(barrier, n_wide * n_grp - 1)

    def send(w, g):
        pltpu.make_async_remote_copy(
            src_ref=send_buf.at[w],
            dst_ref=blocks.at[wide, grp],
            send_sem=send_sems.at[0],
            recv_sem=recv_sems.at[wide],
            device_id=(w, g),
            device_id_type=MESH,
        ).start()

    def send_row(w, g):
        pltpu.make_async_remote_copy(
            src_ref=partial.at[w, g],
            dst_ref=rows_in.at[wide, grp],
            send_sem=send_sems.at[1],
            recv_sem=row_sem,
            device_id=(w, g),
            device_id_type=MESH,
        ).start()

    def wait_all(refs, sem):
        pltpu.make_async_copy(refs, refs, sem).wait()

    loop(n_wide - 1, lambda i: plane(down(wide, i + 1, n_wide), send, 0), 8)
    plane(wide, send, 1)
    blocks[wide, grp] = send_buf[wide]

    loads[2].wait()
    loads[3].wait()
    for a in range(ab_tiles):
        for c in range(cd_tiles):
            block = (slice(a * TW, (a + 1) * TW), slice(c * TW, (c + 1) * TW))
            keep = jnp.full((TW, TW), int_live[a, c].astype(jnp.float32), jnp.float32)
            ints[block] = ints[block] * keep.astype(jnp.bfloat16)

    def multiply(w):
        wide_tiles[...] = blocks[w].astype(jnp.float32).reshape(n_grp * cd_tiles, TW)
        for c in range(cd_tiles):
            lhs[:, c * TW:(c + 1) * TW] = wide_tiles[
                pl.ds(c, n_grp, stride=cd_tiles), :
            ]
        total = lax.dot_general(
            lhs[...].astype(jnp.bfloat16), ints[...], (((1,), (1,)), ((), ())),
            preferred_element_type=jnp.float32,
        )
        partial[w] = total.reshape(n_grp, 1, ab)

    wait_all(blocks.at[0, pl.ds(0, n_grp - 1)], recv_sems.at[wide])
    multiply(wide)
    plane(wide, send_row, 1)
    rows_in[wide, grp] = partial[wide, grp]

    def other_rows(i):
        w = down(wide, i + 1, n_wide)
        wait_all(blocks.at[0], recv_sems.at[w])
        multiply(w)
        plane(w, send_row, 0)

    loop(n_wide - 1, other_rows, 8)

    def wait_others(refs, sem):
        flat = refs.reshape((n_wide * n_grp,) + refs.shape[2:])
        wait_all(flat.at[pl.ds(0, n_wide * n_grp - 1)], sem)

    wait_others(rows_in, row_sem)
    for g in range(n_grp):
        if n_wide <= 8:
            total = rows_in[0, g]
            for w in range(1, n_wide):
                total = total + rows_in[w, g]
        else:
            total = lax.fori_loop(
                1, n_wide, lambda w, s: s + rows_in[w, g], rows_in[0, g]
            )
        out_ref[:, g * ab:(g + 1) * ab] = total.astype(jnp.bfloat16)

    wait_others(blocks, send_sems.at[0])
    wait_others(rows_in, send_sems.at[1])


def per_device(*args):
    amplitudes, amplitude_live, integrals, integral_live = [
        pltpu.with_memory_space_constraint(x, pltpu.HBM) for x in args
    ]
    n_wide = lax.axis_size("wide")
    n_grp = lax.axis_size("grp")
    ab, cd = integrals.shape
    cd_tiles = cd // TW
    bf16, f32 = jnp.bfloat16, jnp.float32
    return pl.pallas_call(
        functools.partial(kernel, n_wide, n_grp),
        out_shape=jax.ShapeDtypeStruct((1, n_grp * ab), bf16),
        in_specs=[pl.BlockSpec(memory_space=pl.ANY)] * 4,
        out_specs=pl.BlockSpec(memory_space=pltpu.VMEM),
        scratch_shapes=[
            pltpu.VMEM(amplitudes.shape, bf16),
            pltpu.SMEM((8, amplitude_live.shape[1]), jnp.int32),
            pltpu.VMEM((ab, cd), bf16),
            pltpu.SMEM(integral_live.shape, jnp.int32),
            pltpu.VMEM((cd_tiles, TW), f32),
            pltpu.VMEM((n_wide, cd_tiles, TW), bf16),
            pltpu.VMEM((n_wide, n_grp, cd_tiles, TW), bf16),
            pltpu.VMEM((n_grp * cd_tiles, TW), f32),
            pltpu.VMEM((n_grp, cd), f32),
            pltpu.VMEM((n_wide, n_grp, 1, ab), f32),
            pltpu.VMEM((n_wide, n_grp, 1, ab), f32),
            pltpu.SemaphoreType.DMA((4,)),
            pltpu.SemaphoreType.DMA((n_wide,)),
            pltpu.SemaphoreType.DMA,
            pltpu.SemaphoreType.DMA((2,)),
        ],
        compiler_params=pltpu.CompilerParams(
            collective_id=0, has_side_effects=True, vmem_limit_bytes=48 * 1024 * 1024
        ),
        cost_estimate=pl.CostEstimate(
            flops=2 * n_wide * n_grp * ab * cd, bytes_accessed=2 * ab * cd, transcendentals=0
        ),
    )(amplitudes, amplitude_live, integrals, integral_live)


def solution(mesh):
    in_specs = (P(("wide", "grp"), None), P(), P("grp", "wide"), P("grp", "wide"))
    out_specs = P(("wide", "grp"), None)
    return jax.shard_map(
        per_device, mesh=mesh, in_specs=in_specs, out_specs=out_specs, check_vma=False
    )
```

```python
import functools

import jax
import jax.numpy as jnp
from jax import lax
from jax.experimental import pallas as pl
from jax.experimental.pallas import tpu as pltpu
from jax.sharding import PartitionSpec as P

TW = 128
MESH = pl.DeviceIdType.MESH


def loop(count, body, limit):
    if count <= limit:
        for i in range(count):
            body(i)
    else:
        lax.fori_loop(0, count, lambda i, c: (body(i), c)[1], 0)


def kernel(
    n_wide, n_grp,
    amp_hbm, live_hbm, int_hbm, int_live_hbm, out_ref,
    amp, live, ints, ints_t, int_live, tiles, send_buf, blocks, wide_tiles, lhs,
    partial, rows_in,
    load_sems, recv_sems, row_sem, send_sems,
):
    ab, cd = ints.shape
    cd_tiles, ab_tiles = cd // TW, ab // TW
    wide = lax.axis_index("wide")
    grp = lax.axis_index("grp")
    my_row = lax.rem(wide * n_grp + grp, 8)

    slab = pl.multiple_of(((wide * n_grp + grp) // 8) * 8, 8)
    loads = [
        pltpu.make_async_copy(amp_hbm, amp, load_sems.at[0]),
        pltpu.make_async_copy(live_hbm.at[pl.ds(slab, 8), :], live, load_sems.at[1]),
        pltpu.make_async_copy(int_live_hbm, int_live, load_sems.at[2]),
        pltpu.make_async_copy(int_hbm, ints, load_sems.at[3]),
    ]
    for load in loads:
        load.start()

    barrier = pltpu.get_barrier_semaphore()

    def up(index, i, count):
        there = index + i
        return jnp.where(there >= count, there - count, there)

    def down(index, i, count):
        there = index - i
        return jnp.where(there < 0, there + count, there)

    near = [up(grp, i, n_grp) for i in range(n_grp)]

    def plane(w, body, first):
        for g in near[first:]:
            body(w, g)

    def greet(w, g):
        pl.semaphore_signal(barrier, inc=1, device_id=(w, g), device_id_type=MESH)

    loop(n_wide - 1, lambda i: plane(up(wide, i + 1, n_wide), greet, 0), 8)
    plane(wide, greet, 1)

    loads[0].wait()
    loads[1].wait()

    def prepare(w):
        for c in range(cd_tiles):
            t = w * cd_tiles + c
            column = t * TW if isinstance(w, int) else pl.multiple_of(t * TW, TW)
            row = amp[:, pl.ds(column, TW)].astype(jnp.float32)
            tiles[c:c + 1, :] = row * live[my_row, t].astype(jnp.float32)
        send_buf[w] = tiles[...].astype(jnp.bfloat16)

    loop(n_wide, prepare, 4)

    pl.semaphore_wait(barrier, n_wide * n_grp - 1)

    def send(w, g):
        pltpu.make_async_remote_copy(
            src_ref=send_buf.at[w],
            dst_ref=blocks.at[wide, grp],
            send_sem=send_sems.at[0],
            recv_sem=recv_sems.at[wide],
            device_id=(w, g),
            device_id_type=MESH,
        ).start()

    def send_row(w, g):
        pltpu.make_async_remote_copy(
            src_ref=partial.at[w, g],
            dst_ref=rows_in.at[wide, grp],
            send_sem=send_sems.at[1],
            recv_sem=row_sem,
            device_id=(w, g),
            device_id_type=MESH,
        ).start()

    def wait_all(refs, sem):
        pltpu.make_async_copy(refs, refs, sem).wait()

    loop(n_wide - 1, lambda i: plane(down(wide, i + 1, n_wide), send, 0), 8)
    plane(wide, send, 1)
    blocks[wide, grp] = send_buf[wide]

    loads[2].wait()
    loads[3].wait()
    for a in range(ab_tiles):
        for c in range(cd_tiles):
            block = (slice(a * TW, (a + 1) * TW), slice(c * TW, (c + 1) * TW))
            keep = jnp.full((TW, TW), int_live[a, c].astype(jnp.float32), jnp.float32)
            ints_t[block[1], block[0]] = (ints[block] * keep.astype(jnp.bfloat16)).T

    def multiply(w):
        wide_tiles[...] = blocks[w].astype(jnp.float32).reshape(n_grp * cd_tiles, TW)
        for c in range(cd_tiles):
            lhs[:, c * TW:(c + 1) * TW] = wide_tiles[
                pl.ds(c, n_grp, stride=cd_tiles), :
            ]
        total = lax.dot_general(
            lhs[...].astype(jnp.bfloat16), ints_t[...], (((1,), (0,)), ((), ())),
            preferred_element_type=jnp.float32,
        )
        partial[w] = total.reshape(n_grp, 1, ab)

    wait_all(blocks.at[0, pl.ds(0, n_grp - 1)], recv_sems.at[wide])
    multiply(wide)
    plane(wide, send_row, 1)
    rows_in[wide, grp] = partial[wide, grp]

    def other_rows(i):
        w = down(wide, i + 1, n_wide)
        wait_all(blocks.at[0], recv_sems.at[w])
        multiply(w)
        plane(w, send_row, 0)

    loop(n_wide - 1, other_rows, 8)

    def wait_others(refs, sem):
        flat = refs.reshape((n_wide * n_grp,) + refs.shape[2:])
        wait_all(flat.at[pl.ds(0, n_wide * n_grp - 1)], sem)

    wait_others(rows_in, row_sem)
    for g in range(n_grp):
        if n_wide <= 8:
            total = rows_in[0, g]
            for w in range(1, n_wide):
                total = total + rows_in[w, g]
        else:
            total = lax.fori_loop(
                1, n_wide, lambda w, s: s + rows_in[w, g], rows_in[0, g]
            )
        out_ref[:, g * ab:(g + 1) * ab] = total.astype(jnp.bfloat16)

    wait_others(blocks, send_sems.at[0])
    wait_others(rows_in, send_sems.at[1])


def per_device(*args):
    amplitudes, amplitude_live, integrals, integral_live = [
        pltpu.with_memory_space_constraint(x, pltpu.HBM) for x in args
    ]
    n_wide = lax.axis_size("wide")
    n_grp = lax.axis_size("grp")
    ab, cd = integrals.shape
    cd_tiles = cd // TW
    bf16, f32 = jnp.bfloat16, jnp.float32
    return pl.pallas_call(
        functools.partial(kernel, n_wide, n_grp),
        out_shape=jax.ShapeDtypeStruct((1, n_grp * ab), bf16),
        in_specs=[pl.BlockSpec(memory_space=pl.ANY)] * 4,
        out_specs=pl.BlockSpec(memory_space=pltpu.VMEM),
        scratch_shapes=[
            pltpu.VMEM(amplitudes.shape, bf16),
            pltpu.SMEM((8, amplitude_live.shape[1]), jnp.int32),
            pltpu.VMEM((ab, cd), bf16),
            pltpu.VMEM((cd, ab), bf16),
            pltpu.SMEM(integral_live.shape, jnp.int32),
            pltpu.VMEM((cd_tiles, TW), f32),
            pltpu.VMEM((n_wide, cd_tiles, TW), bf16),
            pltpu.VMEM((n_wide, n_grp, cd_tiles, TW), bf16),
            pltpu.VMEM((n_grp * cd_tiles, TW), f32),
            pltpu.VMEM((n_grp, cd), f32),
            pltpu.VMEM((n_wide, n_grp, 1, ab), f32),
            pltpu.VMEM((n_wide, n_grp, 1, ab), f32),
            pltpu.SemaphoreType.DMA((4,)),
            pltpu.SemaphoreType.DMA((n_wide,)),
            pltpu.SemaphoreType.DMA,
            pltpu.SemaphoreType.DMA((2,)),
        ],
        compiler_params=pltpu.CompilerParams(
            collective_id=0, has_side_effects=True, vmem_limit_bytes=48 * 1024 * 1024
        ),
        cost_estimate=pl.CostEstimate(
            flops=2 * n_wide * n_grp * ab * cd, bytes_accessed=2 * ab * cd, transcendentals=0
        ),
    )(amplitudes, amplitude_live, integrals, integral_live)


def solution(mesh):
    in_specs = (P(("wide", "grp"), None), P(), P("grp", "wide"), P("grp", "wide"))
    out_specs = P(("wide", "grp"), None)
    return jax.shard_map(
        per_device, mesh=mesh, in_specs=in_specs, out_specs=out_specs, check_vma=False
    )
```

```python
import functools

import jax
import jax.numpy as jnp
from jax import lax
from jax.experimental import pallas as pl
from jax.experimental.pallas import tpu as pltpu
from jax.sharding import PartitionSpec as P

TW = 128
MESH = pl.DeviceIdType.MESH


def loop(count, body, limit):
    if count <= limit:
        for i in range(count):
            body(i)
    else:
        lax.fori_loop(0, count, lambda i, c: (body(i), c)[1], 0)


def kernel(
    n_wide, n_grp,
    amp_hbm, live_hbm, int_hbm, int_live_hbm, out_ref,
    amp, live, ints, ints_t, int_live, tiles, send_buf, blocks, wide_tiles, lhs,
    partial, rows_in,
    load_sems, send_sems, recv_sems,
):
    ab, cd = ints.shape
    cd_tiles, ab_tiles = cd // TW, ab // TW
    wide = lax.axis_index("wide")
    grp = lax.axis_index("grp")
    my_row = lax.rem(wide * n_grp + grp, 8)

    slab = pl.multiple_of(((wide * n_grp + grp) // 8) * 8, 8)
    loads = [
        pltpu.make_async_copy(amp_hbm, amp, load_sems.at[0]),
        pltpu.make_async_copy(live_hbm.at[pl.ds(slab, 8), :], live, load_sems.at[1]),
        pltpu.make_async_copy(int_live_hbm, int_live, load_sems.at[2]),
        pltpu.make_async_copy(int_hbm, ints, load_sems.at[3]),
    ]
    for load in loads:
        load.start()

    barrier = pltpu.get_barrier_semaphore()

    def up(index, i, count):
        there = index + i
        return jnp.where(there >= count, there - count, there)

    def down(index, i, count):
        there = index - i
        return jnp.where(there < 0, there + count, there)

    near = [up(grp, i, n_grp) for i in range(n_grp)]

    def plane(w, body, first):
        for g in near[first:]:
            body(w, g)

    def greet(w, g):
        pl.semaphore_signal(barrier, inc=1, device_id=(w, g), device_id_type=MESH)

    loop(n_wide - 1, lambda i: greet(up(wide, i + 1, n_wide), grp), 8)
    plane(wide, greet, 1)

    loads[0].wait()
    loads[1].wait()

    def prepare(w):
        for c in range(cd_tiles):
            t = w * cd_tiles + c
            column = t * TW if isinstance(w, int) else pl.multiple_of(t * TW, TW)
            row = amp[:, pl.ds(column, TW)].astype(jnp.float32)
            tiles[c:c + 1, :] = row * live[my_row, t].astype(jnp.float32)
        send_buf[w] = tiles[...].astype(jnp.bfloat16)

    loop(n_wide, prepare, 4)

    pl.semaphore_wait(barrier, n_wide + n_grp - 2)

    def send_block(w):
        pltpu.make_async_remote_copy(
            src_ref=send_buf.at[w],
            dst_ref=blocks.at[grp, wide],
            send_sem=send_sems.at[0],
            recv_sem=recv_sems.at[0],
            device_id=(w, grp),
            device_id_type=MESH,
        ).start()

    def send_column(w, g):
        pltpu.make_async_remote_copy(
            src_ref=blocks.at[grp],
            dst_ref=blocks.at[grp],
            send_sem=send_sems.at[1],
            recv_sem=recv_sems.at[1],
            device_id=(w, g),
            device_id_type=MESH,
        ).start()

    def send_row(w, g):
        pltpu.make_async_remote_copy(
            src_ref=partial.at[g * n_wide + w],
            dst_ref=rows_in.at[wide * n_grp + grp],
            send_sem=send_sems.at[2],
            recv_sem=recv_sems.at[2],
            device_id=(w, g),
            device_id_type=MESH,
        ).start()

    def wait_all(refs, sem):
        pltpu.make_async_copy(refs, refs, sem).wait()

    loop(n_wide - 1, lambda i: send_block(down(wide, i + 1, n_wide)), 8)
    blocks[grp, wide] = send_buf[wide]
    from_wide = blocks.at[0, pl.ds(0, n_wide - 1)]
    wait_all(from_wide, recv_sems.at[0])
    plane(wide, send_column, 1)

    loads[2].wait()
    loads[3].wait()
    for a in range(ab_tiles):
        for c in range(cd_tiles):
            block = (slice(a * TW, (a + 1) * TW), slice(c * TW, (c + 1) * TW))
            keep = jnp.full((TW, TW), int_live[a, c].astype(jnp.float32), jnp.float32)
            ints_t[block[1], block[0]] = (ints[block] * keep.astype(jnp.bfloat16)).T

    from_grp = blocks.at[pl.ds(0, n_grp - 1)]
    wait_all(from_grp, recv_sems.at[1])

    n = n_wide * n_grp
    step = lhs.shape[0]
    flat = blocks.reshape(n, cd_tiles, TW)

    def multiply(i):
        here = pl.ds(i * step, step)
        wide_tiles[...] = flat[here].astype(jnp.float32).reshape(step * cd_tiles, TW)
        for c in range(cd_tiles):
            lhs[:, c * TW:(c + 1) * TW] = wide_tiles[
                pl.ds(c, step, stride=cd_tiles), :
            ].astype(jnp.bfloat16)
        total = lax.dot_general(
            lhs[...], ints_t[...], (((1,), (0,)), ((), ())),
            preferred_element_type=jnp.float32,
        )
        partial[here] = total.reshape(step, 1, ab)

    loop(n // step, multiply, 1)

    loop(n_wide - 1, lambda i: plane(down(wide, i + 1, n_wide), send_row, 0), 8)
    plane(wide, send_row, 1)
    rows_in[wide * n_grp + grp] = partial[grp * n_wide + wide]
    from_others = rows_in.at[pl.ds(0, n - 1)]
    wait_all(from_others, recv_sems.at[2])
    for g in range(n_grp):
        if n_wide <= 8:
            total = rows_in[g]
            for w in range(1, n_wide):
                total = total + rows_in[w * n_grp + g]
        else:
            total = lax.fori_loop(
                1, n_wide, lambda w, s: s + rows_in[w * n_grp + g], rows_in[g]
            )
        out_ref[:, g * ab:(g + 1) * ab] = total.astype(jnp.bfloat16)

    wait_all(from_wide, send_sems.at[0])
    wait_all(from_grp, send_sems.at[1])
    wait_all(from_others, send_sems.at[2])


def per_device(*args):
    amplitudes, amplitude_live, integrals, integral_live = [
        pltpu.with_memory_space_constraint(x, pltpu.HBM) for x in args
    ]
    n_wide = lax.axis_size("wide")
    n_grp = lax.axis_size("grp")
    ab, cd = integrals.shape
    cd_tiles = cd // TW
    n = n_wide * n_grp
    step = min(n, 32)
    bf16, f32 = jnp.bfloat16, jnp.float32
    return pl.pallas_call(
        functools.partial(kernel, n_wide, n_grp),
        out_shape=jax.ShapeDtypeStruct((1, n_grp * ab), bf16),
        in_specs=[pl.BlockSpec(memory_space=pl.ANY)] * 4,
        out_specs=pl.BlockSpec(memory_space=pltpu.VMEM),
        scratch_shapes=[
            pltpu.VMEM(amplitudes.shape, bf16),
            pltpu.SMEM((8, amplitude_live.shape[1]), jnp.int32),
            pltpu.VMEM((ab, cd), bf16),
            pltpu.VMEM((cd, ab), bf16),
            pltpu.SMEM(integral_live.shape, jnp.int32),
            pltpu.VMEM((cd_tiles, TW), f32),
            pltpu.VMEM((n_wide, cd_tiles, TW), bf16),
            pltpu.VMEM((n_grp, n_wide, cd_tiles, TW), bf16),
            pltpu.VMEM((step * cd_tiles, TW), f32),
            pltpu.VMEM((step, cd), bf16),
            pltpu.VMEM((n, 1, ab), f32),
            pltpu.VMEM((n, 1, ab), f32),
            pltpu.SemaphoreType.DMA((4,)),
            pltpu.SemaphoreType.DMA((3,)),
            pltpu.SemaphoreType.DMA((3,)),
        ],
        compiler_params=pltpu.CompilerParams(
            collective_id=0, has_side_effects=True, vmem_limit_bytes=48 * 1024 * 1024
        ),
        cost_estimate=pl.CostEstimate(
            flops=2 * n_wide * n_grp * ab * cd, bytes_accessed=2 * ab * cd, transcendentals=0
        ),
    )(amplitudes, amplitude_live, integrals, integral_live)


def solution(mesh):
    in_specs = (P(("wide", "grp"), None), P(), P("grp", "wide"), P("grp", "wide"))
    out_specs = P(("wide", "grp"), None)
    return jax.shard_map(
        per_device, mesh=mesh, in_specs=in_specs, out_specs=out_specs, check_vma=False
    )
```

```python
import functools

import jax
import jax.numpy as jnp
from jax import lax
from jax.experimental import pallas as pl
from jax.experimental.pallas import tpu as pltpu
from jax.sharding import PartitionSpec as P

TW = 128
MESH = pl.DeviceIdType.MESH


def loop(count, body, limit):
    if count <= limit:
        for i in range(count):
            body(i)
    else:
        lax.fori_loop(0, count, lambda i, c: (body(i), c)[1], 0)


def kernel(
    n_wide, n_grp,
    amp_hbm, live_hbm, int_hbm, int_live_hbm, out_ref,
    amp, live, ints, ints_t, int_live, tiles, send_buf, blocks, wide_tiles, lhs,
    partial, rows_in,
    load_sems, send_sems, recv_sems, column_sems,
):
    ab, cd = ints.shape
    cd_tiles, ab_tiles = cd // TW, ab // TW
    wide = lax.axis_index("wide")
    grp = lax.axis_index("grp")
    my_row = lax.rem(wide * n_grp + grp, 8)

    slab = pl.multiple_of(((wide * n_grp + grp) // 8) * 8, 8)
    loads = [
        pltpu.make_async_copy(amp_hbm, amp, load_sems.at[0]),
        pltpu.make_async_copy(live_hbm.at[pl.ds(slab, 8), :], live, load_sems.at[1]),
        pltpu.make_async_copy(int_live_hbm, int_live, load_sems.at[2]),
        pltpu.make_async_copy(int_hbm, ints, load_sems.at[3]),
    ]
    loads[0].start()
    loads[1].start()

    barrier = pltpu.get_barrier_semaphore()

    def up(index, i, count):
        there = index + i
        return jnp.where(there >= count, there - count, there)

    def down(index, i, count):
        there = index - i
        return jnp.where(there < 0, there + count, there)

    near = [up(grp, i, n_grp) for i in range(n_grp)]

    def plane(w, body, first):
        for g in near[first:]:
            body(w, g)

    def greet(w, g):
        pl.semaphore_signal(barrier, inc=1, device_id=(w, g), device_id_type=MESH)

    loop(n_wide - 1, lambda i: greet(up(wide, i + 1, n_wide), grp), 8)
    plane(wide, greet, 1)
    loads[2].start()
    loads[3].start()

    loads[0].wait()
    loads[1].wait()

    def prepare(w):
        for c in range(cd_tiles):
            t = w * cd_tiles + c
            column = t * TW if isinstance(w, int) else pl.multiple_of(t * TW, TW)
            row = amp[:, pl.ds(column, TW)].astype(jnp.float32)
            tiles[c:c + 1, :] = row * live[my_row, t].astype(jnp.float32)
        send_buf[w] = tiles[...].astype(jnp.bfloat16)

    loop(n_wide, prepare, 4)

    pl.semaphore_wait(barrier, n_wide + n_grp - 2)

    def send_block(w):
        pltpu.make_async_remote_copy(
            src_ref=send_buf.at[w],
            dst_ref=blocks.at[grp, wide],
            send_sem=send_sems.at[0],
            recv_sem=recv_sems.at[0],
            device_id=(w, grp),
            device_id_type=MESH,
        ).start()

    def send_column(w, g):
        pltpu.make_async_remote_copy(
            src_ref=blocks.at[grp],
            dst_ref=blocks.at[grp],
            send_sem=send_sems.at[1],
            recv_sem=column_sems.at[grp],
            device_id=(w, g),
            device_id_type=MESH,
        ).start()

    def send_row(w, i):
        pltpu.make_async_remote_copy(
            src_ref=partial.at[i * n_wide + w],
            dst_ref=rows_in.at[wide * n_grp + grp],
            send_sem=send_sems.at[2],
            recv_sem=recv_sems.at[2],
            device_id=(w, near[i]),
            device_id_type=MESH,
        ).start()

    def wait_all(refs, sem):
        pltpu.make_async_copy(refs, refs, sem).wait()

    loop(n_wide - 1, lambda i: send_block(down(wide, i + 1, n_wide)), 8)
    blocks[grp, wide] = send_buf[wide]
    from_wide = blocks.at[0, pl.ds(0, n_wide - 1)]
    wait_all(from_wide, recv_sems.at[0])
    plane(wide, send_column, 1)

    loads[2].wait()
    loads[3].wait()
    for a in range(ab_tiles):
        for c in range(cd_tiles):
            block = (slice(a * TW, (a + 1) * TW), slice(c * TW, (c + 1) * TW))
            keep = jnp.full((TW, TW), int_live[a, c].astype(jnp.float32), jnp.float32)
            ints_t[block[1], block[0]] = (ints[block] * keep.astype(jnp.bfloat16)).T

    for i, g in enumerate(near):
        if i > 0:
            wait_all(blocks.at[0], column_sems.at[g])
        wide_tiles[i] = blocks[g].astype(jnp.float32).reshape(n_wide * cd_tiles, TW)
        for c in range(cd_tiles):
            lhs[i * n_wide:(i + 1) * n_wide, c * TW:(c + 1) * TW] = wide_tiles[
                i, pl.ds(c, n_wide, stride=cd_tiles), :
            ]

    n = n_wide * n_grp
    step = min(n, 32)
    from_grp = blocks.at[pl.ds(0, n_grp - 1)]

    def multiply(i):
        here = pl.ds(i * step, step)
        total = lax.dot_general(
            lhs[here].astype(jnp.bfloat16), ints_t[...], (((1,), (0,)), ((), ())),
            preferred_element_type=jnp.float32,
        )
        partial[here] = total.reshape(step, 1, ab)

    loop(n // step, multiply, 1)

    def send_rows(w, first):
        for i in range(first, n_grp):
            send_row(w, i)

    loop(n_wide - 1, lambda j: send_rows(down(wide, j + 1, n_wide), 0), 8)
    send_rows(wide, 1)
    rows_in[wide * n_grp + grp] = partial[wide]
    from_others = rows_in.at[pl.ds(0, n - 1)]
    wait_all(from_others, recv_sems.at[2])
    for g in range(n_grp):
        if n_wide <= 8:
            total = rows_in[g]
            for w in range(1, n_wide):
                total = total + rows_in[w * n_grp + g]
        else:
            total = lax.fori_loop(
                1, n_wide, lambda w, s: s + rows_in[w * n_grp + g], rows_in[g]
            )
        out_ref[:, g * ab:(g + 1) * ab] = total.astype(jnp.bfloat16)

    wait_all(from_wide, send_sems.at[0])
    wait_all(from_grp, send_sems.at[1])
    wait_all(from_others, send_sems.at[2])


def per_device(*args):
    amplitudes, amplitude_live, integrals, integral_live = [
        pltpu.with_memory_space_constraint(x, pltpu.HBM) for x in args
    ]
    n_wide = lax.axis_size("wide")
    n_grp = lax.axis_size("grp")
    ab, cd = integrals.shape
    cd_tiles = cd // TW
    n = n_wide * n_grp
    bf16, f32 = jnp.bfloat16, jnp.float32
    return pl.pallas_call(
        functools.partial(kernel, n_wide, n_grp),
        out_shape=jax.ShapeDtypeStruct((1, n_grp * ab), bf16),
        in_specs=[pl.BlockSpec(memory_space=pl.ANY)] * 4,
        out_specs=pl.BlockSpec(memory_space=pltpu.VMEM),
        scratch_shapes=[
            pltpu.VMEM(amplitudes.shape, bf16),
            pltpu.SMEM((8, amplitude_live.shape[1]), jnp.int32),
            pltpu.VMEM((ab, cd), bf16),
            pltpu.VMEM((cd, ab), bf16),
            pltpu.SMEM(integral_live.shape, jnp.int32),
            pltpu.VMEM((cd_tiles, TW), f32),
            pltpu.VMEM((n_wide, cd_tiles, TW), bf16),
            pltpu.VMEM((n_grp, n_wide, cd_tiles, TW), bf16),
            pltpu.VMEM((n_grp, n_wide * cd_tiles, TW), f32),
            pltpu.VMEM((n, cd), f32),
            pltpu.VMEM((n, 1, ab), f32),
            pltpu.VMEM((n, 1, ab), f32),
            pltpu.SemaphoreType.DMA((4,)),
            pltpu.SemaphoreType.DMA((3,)),
            pltpu.SemaphoreType.DMA((3,)),
            pltpu.SemaphoreType.DMA((n_grp,)),
        ],
        compiler_params=pltpu.CompilerParams(
            collective_id=0, has_side_effects=True, vmem_limit_bytes=48 * 1024 * 1024
        ),
        cost_estimate=pl.CostEstimate(
            flops=2 * n_wide * n_grp * ab * cd, bytes_accessed=2 * ab * cd, transcendentals=0
        ),
    )(amplitudes, amplitude_live, integrals, integral_live)


def solution(mesh):
    in_specs = (P(("wide", "grp"), None), P(), P("grp", "wide"), P("grp", "wide"))
    out_specs = P(("wide", "grp"), None)
    return jax.shard_map(
        per_device, mesh=mesh, in_specs=in_specs, out_specs=out_specs, check_vma=False
    )
```

```python
import functools

import jax
import jax.numpy as jnp
from jax import lax
from jax.experimental import pallas as pl
from jax.experimental.pallas import tpu as pltpu
from jax.sharding import PartitionSpec as P

TW = 128
MESH = pl.DeviceIdType.MESH


def loop(count, body, limit):
    if count <= limit:
        for i in range(count):
            body(i)
    else:
        lax.fori_loop(0, count, lambda i, c: (body(i), c)[1], 0)


def kernel(
    n_wide, n_grp,
    amp_hbm, live_hbm, int_hbm, int_live_hbm, out_ref,
    amp, live, ints, ints_t, int_live, tiles, send_buf, blocks, wide_tiles, lhs,
    partial, rows_in,
    load_sems, recv_sems, row_sem, forward_sems, send_sems,
):
    ab, cd = ints.shape
    cd_tiles, ab_tiles = cd // TW, ab // TW
    wide = lax.axis_index("wide")
    grp = lax.axis_index("grp")
    my_row = lax.rem(wide * n_grp + grp, 8)

    slab = pl.multiple_of(((wide * n_grp + grp) // 8) * 8, 8)
    loads = [
        pltpu.make_async_copy(amp_hbm, amp, load_sems.at[0]),
        pltpu.make_async_copy(live_hbm.at[pl.ds(slab, 8), :], live, load_sems.at[1]),
        pltpu.make_async_copy(int_live_hbm, int_live, load_sems.at[2]),
        pltpu.make_async_copy(int_hbm, ints, load_sems.at[3]),
    ]
    for load in loads:
        load.start()

    barrier = pltpu.get_barrier_semaphore()

    def up(index, i, count):
        there = index + i
        return jnp.where(there >= count, there - count, there)

    def down(index, i, count):
        there = index - i
        return jnp.where(there < 0, there + count, there)

    half = n_grp // 2
    core, chip = lax.rem(grp, 2), grp // 2
    near = [up(grp, i, n_grp) for i in range(n_grp)]
    same_core = [up(chip, i, half) * 2 + core for i in range(half)]
    partner = chip * 2 + 1 - core

    def greet(w, g):
        pl.semaphore_signal(barrier, inc=1, device_id=(w, g), device_id_type=MESH)

    def plane(w, body, first):
        for g in same_core[first:]:
            body(w, g)

    loop(n_wide - 1, lambda i: plane(up(wide, i + 1, n_wide), greet, 0), 8)
    plane(wide, greet, 1)
    greet(wide, partner)

    loads[0].wait()
    loads[1].wait()

    def prepare(w):
        for c in range(cd_tiles):
            t = w * cd_tiles + c
            column = t * TW if isinstance(w, int) else pl.multiple_of(t * TW, TW)
            row = amp[:, pl.ds(column, TW)].astype(jnp.float32)
            tiles[c:c + 1, :] = row * live[my_row, t].astype(jnp.float32)
        send_buf[w] = tiles[...].astype(jnp.bfloat16)

    loop(n_wide, prepare, 4)

    pl.semaphore_wait(barrier, n_wide * half)

    def send(w, g):
        pltpu.make_async_remote_copy(
            src_ref=send_buf.at[w],
            dst_ref=blocks.at[wide, core, chip],
            send_sem=send_sems.at[0],
            recv_sem=recv_sems.at[wide],
            device_id=(w, g),
            device_id_type=MESH,
        ).start()

    def forward(w):
        pltpu.make_async_remote_copy(
            src_ref=blocks.at[w, core],
            dst_ref=blocks.at[w, core],
            send_sem=send_sems.at[2],
            recv_sem=forward_sems.at[w],
            device_id=(wide, partner),
            device_id_type=MESH,
        ).start()

    def send_row(w, g):
        pltpu.make_async_remote_copy(
            src_ref=partial.at[w, lax.rem(g, 2) * half + g // 2],
            dst_ref=rows_in.at[wide, grp],
            send_sem=send_sems.at[1],
            recv_sem=row_sem,
            device_id=(w, g),
            device_id_type=MESH,
        ).start()

    def wait_all(refs, sem):
        pltpu.make_async_copy(refs, refs, sem).wait()

    loop(n_wide - 1, lambda i: plane(down(wide, i + 1, n_wide), send, 0), 8)
    plane(wide, send, 1)
    blocks[wide, core, chip] = send_buf[wide]

    loads[2].wait()
    loads[3].wait()
    for a in range(ab_tiles):
        for c in range(cd_tiles):
            block = (slice(a * TW, (a + 1) * TW), slice(c * TW, (c + 1) * TW))
            keep = jnp.full((TW, TW), int_live[a, c].astype(jnp.float32), jnp.float32)
            ints_t[block[1], block[0]] = (ints[block] * keep.astype(jnp.bfloat16)).T

    def multiply(w):
        wide_tiles[...] = blocks[w].astype(jnp.float32).reshape(n_grp * cd_tiles, TW)
        for c in range(cd_tiles):
            lhs[:, c * TW:(c + 1) * TW] = wide_tiles[
                pl.ds(c, n_grp, stride=cd_tiles), :
            ]
        total = lax.dot_general(
            lhs[...].astype(jnp.bfloat16), ints_t[...], (((1,), (0,)), ((), ())),
            preferred_element_type=jnp.float32,
        )
        partial[w] = total.reshape(n_grp, 1, ab)

    def finish(w, first):
        wait_all(blocks.at[0, 0], forward_sems.at[w])
        multiply(w)
        for g in near[first:]:
            send_row(w, g)

    def arrive(i):
        w = down(wide, i, n_wide)
        wait_all(blocks.at[0, 0], recv_sems.at[w])
        forward(w)

    wait_all(blocks.at[0, 0, pl.ds(0, half - 1)], recv_sems.at[wide])
    forward(wide)
    arrive(1)
    finish(wide, 1)
    rows_in[wide, grp] = partial[wide, core * half + chip]

    def other_rows(i):
        arrive(i + 2)
        finish(down(wide, i + 1, n_wide), 0)

    loop(n_wide - 2, other_rows, 8)
    finish(down(wide, n_wide - 1, n_wide), 0)

    n = n_wide * n_grp
    others = rows_in.reshape(n, 1, ab).at[pl.ds(0, n - 1)]
    wait_all(others, row_sem)
    for g in range(n_grp):
        if n_wide <= 8:
            total = rows_in[0, g]
            for w in range(1, n_wide):
                total = total + rows_in[w, g]
        else:
            total = lax.fori_loop(
                1, n_wide, lambda w, s: s + rows_in[w, g], rows_in[0, g]
            )
        out_ref[:, g * ab:(g + 1) * ab] = total.astype(jnp.bfloat16)

    sent = blocks.reshape(n, cd_tiles, TW)
    wait_all(sent.at[pl.ds(0, n // 2 - 1)], send_sems.at[0])
    wait_all(others, send_sems.at[1])
    wait_all(sent.at[pl.ds(0, n // 2)], send_sems.at[2])


def per_device(*args):
    amplitudes, amplitude_live, integrals, integral_live = [
        pltpu.with_memory_space_constraint(x, pltpu.HBM) for x in args
    ]
    n_wide = lax.axis_size("wide")
    n_grp = lax.axis_size("grp")
    ab, cd = integrals.shape
    cd_tiles = cd // TW
    bf16, f32 = jnp.bfloat16, jnp.float32
    return pl.pallas_call(
        functools.partial(kernel, n_wide, n_grp),
        out_shape=jax.ShapeDtypeStruct((1, n_grp * ab), bf16),
        in_specs=[pl.BlockSpec(memory_space=pl.ANY)] * 4,
        out_specs=pl.BlockSpec(memory_space=pltpu.VMEM),
        scratch_shapes=[
            pltpu.VMEM(amplitudes.shape, bf16),
            pltpu.SMEM((8, amplitude_live.shape[1]), jnp.int32),
            pltpu.VMEM((ab, cd), bf16),
            pltpu.VMEM((cd, ab), bf16),
            pltpu.SMEM(integral_live.shape, jnp.int32),
            pltpu.VMEM((cd_tiles, TW), f32),
            pltpu.VMEM((n_wide, cd_tiles, TW), bf16),
            pltpu.VMEM((n_wide, 2, n_grp // 2, cd_tiles, TW), bf16),
            pltpu.VMEM((n_grp * cd_tiles, TW), f32),
            pltpu.VMEM((n_grp, cd), f32),
            pltpu.VMEM((n_wide, n_grp, 1, ab), f32),
            pltpu.VMEM((n_wide, n_grp, 1, ab), f32),
            pltpu.SemaphoreType.DMA((4,)),
            pltpu.SemaphoreType.DMA((n_wide,)),
            pltpu.SemaphoreType.DMA,
            pltpu.SemaphoreType.DMA((n_wide,)),
            pltpu.SemaphoreType.DMA((3,)),
        ],
        compiler_params=pltpu.CompilerParams(
            collective_id=0, has_side_effects=True, vmem_limit_bytes=48 * 1024 * 1024
        ),
        cost_estimate=pl.CostEstimate(
            flops=2 * n_wide * n_grp * ab * cd, bytes_accessed=2 * ab * cd, transcendentals=0
        ),
    )(amplitudes, amplitude_live, integrals, integral_live)


def solution(mesh):
    in_specs = (P(("wide", "grp"), None), P(), P("grp", "wide"), P("grp", "wide"))
    out_specs = P(("wide", "grp"), None)
    return jax.shard_map(
        per_device, mesh=mesh, in_specs=in_specs, out_specs=out_specs, check_vma=False
    )
```
